32 devices in a mesh: seq: 8 (over z, x), dp: 4 (over y, core).
Axes of the slice: x: 2, y: 2, z: 4, core: 2. Of those that a mesh axis runs over, the one named last changes fastest.
Arguments:
- hidden_in: bfloat16 [8, 2048, 768], P('dp', 'seq'), may hold values from -6 to 6
- cotangent: bfloat16 [8, 2048, 768], P('dp', 'seq'), may hold values from -6 to 6
- w_qkv: float32 [768, 2304], P('dp'), may hold values from -0.3125 to 0.3125
- w_out: float32 [768, 768], P('dp'), may hold values from -0.75 to 0.75
- pool_kernel: float32 [2, 5, 768], replicated, may hold values from -3 to 3
- norm1_gain: float32 [768], replicated, may hold values from 0.5 to 1.5
- norm1_bias: float32 [768], replicated, may hold values from -1.5 to 1.5
- w_up: float32 [768, 3072], P('dp'), may hold values from -0.21875 to 0.21875
- up_bias: float32 [3072], replicated, may hold values from -2.5 to 2.5
- w_down: float32 [3072, 768], P('dp'), may hold values from -0.15625 to 0.15625
- down_bias: float32 [768], replicated, may hold values from -1.5 to 1.5
- norm2_gain: float32 [768], replicated, may hold values from 0.5 to 1.5
- norm2_bias: float32 [768], replicated, may hold values from -1.5 to 1.5
- doc_lengths: int32 [8, 2], P('dp'), may hold values from 0 to 2048, as said below
- doc_offsets: int32 [8, 2], P('dp'), may hold values from 0 to 2048, as said below
Outputs:
- block_out: float32 [8, 2048, 768], P('dp', 'seq')
- grad_in: float32 [8, 2048, 768], P('dp', 'seq')
- grad_w_qkv: float32 [768, 2304], P('dp')
- grad_w_out: float32 [768, 768], P('dp')
- grad_pool_kernel: float32 [2, 5, 768], replicated
- grad_norm1_gain: float32 [768], replicated
- grad_norm1_bias: float32 [768], replicated
- grad_w_up: float32 [768, 3072], P('dp')
- grad_up_bias: float32 [3072], replicated
- grad_w_down: float32 [3072, 768], P('dp')
- grad_down_bias: float32 [768], replicated
- grad_norm2_gain: float32 [768], replicated
- grad_norm2_bias: float32 [768], replicated
The draws below stay inside these ranges and needn't reach their ends.
Inputs may be any that keep to these rules, and one draw needn't show every extreme that they name: Slot j of a row gives document j: it occupies tokens doc_offsets[j] to doc_offsets[j] + doc_lengths[j] - 1 of the row. Lengths are multiples of 4; documents lie in rising order without intersection, each starts at a multiple of 128, the first at 0; an unused slot has length 0 and offset 2048. Of the 2 rows of each index of dp, one is a single document of 2048 tokens. `doc_offsets`: the starts of the documents given by doc_lengths.
All inputs are finite; a program needn't handle non-finite values.
Results may differ from the reference program's by a relative error of at most 0.018.
The reference program's roundings to bfloat16 on the way count: a program that leaves them out, or rounds other values in their place, can miss the bound.
Values may be sent and summed in bfloat16 or wider, within the bound.
No kernel may reach another device: no remote copies, remote signals or barrier semaphores. Data moves between devices by JAX's collectives and lax.ppermute only.
A program may use at most 192 MiB of HBM per device.

```python
import jax
import jax.numpy as jnp
from jax import lax

D = 768
HEAD = 64
FF = 3072
WIN = 128
PWIN = 512
BLOCK = 128
DOCMIN = 1024
ROWS_DEV = 2
SEQ = 2048
ROWS = 8
NDOC = 2


def doc_layout(key):
    key_len, key_gap, key_long = jax.random.split(key, 3)
    slot_index = jnp.arange(NDOC, dtype=jnp.int32)[None, :]
    doc_len = DOCMIN + 4 * jax.random.randint(key_len, (ROWS, NDOC), 0, DOCMIN // 4 + 1, dtype=jnp.int32)
    gap_blocks = BLOCK * jax.random.randint(key_gap, (ROWS, NDOC), 0, 3, dtype=jnp.int32)
    footprint = (doc_len + BLOCK - 1) // BLOCK * BLOCK + gap_blocks
    doc_start = jnp.cumsum(footprint, axis=1) - footprint
    in_row = doc_start < SEQ
    doc_len = jnp.where(in_row, jnp.minimum(doc_len, SEQ - doc_start), 0)
    doc_start = jnp.where(in_row, doc_start, SEQ)
    groups = ROWS // ROWS_DEV
    long_pick = jax.random.randint(key_long, (groups,), 0, ROWS_DEV, dtype=jnp.int32)
    row_index = jnp.arange(ROWS, dtype=jnp.int32)
    long_row = (row_index % ROWS_DEV == long_pick[row_index // ROWS_DEV])[:, None]
    doc_len = jnp.where(long_row, jnp.where(slot_index == 0, SEQ, 0), doc_len)
    doc_start = jnp.where(long_row, jnp.where(slot_index == 0, 0, SEQ), doc_start)
    return (doc_len.astype(jnp.int32), doc_start.astype(jnp.int32))


def draw_doc_lengths(key, part):
    return doc_layout(key)[0]


def draw_doc_offsets(key, part):
    return doc_layout(key)[1]


def block_scale(rng, shape, pieces, smallest, high):
    gain = 1.0
    for position, shards_of in pieces:
        heights = jax.random.uniform(jax.random.fold_in(jax.random.fold_in(rng, 6), position), (shards_of,), jnp.float32, smallest / len(pieces), high / len(pieces))
        gain = gain * jnp.repeat(jnp.exp(heights), shape[position] // shards_of).reshape((-1,) + (1,) * (len(shape) - 1 - position))
    return gain


def scatter_about(own_key, dims, scale, limit, cuts=(), kind=jnp.bfloat16):
    drawn = scale * jax.random.normal(own_key, dims, jnp.float32)
    if cuts:
        drawn = drawn * block_scale(own_key, dims, cuts, -0.22, 0.18)
    return jnp.clip(drawn, -limit, limit).astype(kind)


def setup_inputs(seed: int = 0) -> dict:
    seeds = jax.random.split(jax.random.key(seed), 16)
    return {
        "hidden_in": scatter_about(seeds[0], (ROWS, SEQ, D), 1.0, 6.0, ((0, 4), (1, 8))),
        "cotangent": scatter_about(seeds[1], (ROWS, SEQ, D), 1.0, 6.0, ((0, 4), (1, 8))),
        "w_qkv": scatter_about(seeds[2], (D, 3 * D), (D // 2) ** -0.5, 0.3125, ((0, 4),), jnp.float32),
        "w_out": scatter_about(seeds[3], (D, D), (D // 12) ** -0.5, 0.75, ((0, 4),), jnp.float32),
        "pool_kernel": scatter_about(seeds[4], (2, 5, D), 0.45, 3.0, (), jnp.float32),
        "norm1_gain": jnp.clip(1.0 + 0.1 * jax.random.normal(seeds[5], (D,), jnp.float32), 0.5, 1.5),
        "norm1_bias": scatter_about(seeds[6], (D,), 0.3, 1.5, (), jnp.float32),
        "w_up": scatter_about(seeds[7], (D, FF), D ** -0.5, 0.21875, ((0, 4),), jnp.float32),
        "up_bias": scatter_about(seeds[8], (FF,), 0.5, 2.5, (), jnp.float32),
        "w_down": scatter_about(seeds[9], (FF, D), (FF // 2) ** -0.5, 0.15625, ((0, 4),), jnp.float32),
        "down_bias": scatter_about(seeds[10], (D,), 0.3, 1.5, (), jnp.float32),
        "norm2_gain": jnp.clip(1.0 + 0.1 * jax.random.normal(seeds[11], (D,), jnp.float32), 0.5, 1.5),
        "norm2_bias": scatter_about(seeds[12], (D,), 0.3, 1.5, (), jnp.float32),
        "doc_lengths": draw_doc_lengths(jax.random.fold_in(seeds[15], 71), 0),
        "doc_offsets": draw_doc_offsets(jax.random.fold_in(seeds[15], 71), 0),
    }


precise = lax.Precision.HIGHEST
epsilon = 1e-05

@jax.custom_vjp
def low(v):
    return lax.optimization_barrier(v.astype(jnp.bfloat16)).astype(jnp.float32)

@jax.custom_vjp
def low_back(v):
    return v

def low_keep(v):
    return (low(v), None)

def low_pass(kept, grad):
    return (grad,)

def back_keep(v):
    return (v, None)

def back_low(kept, grad):
    return (low(grad),)
low.defvjp(low_keep, low_pass)
low_back.defvjp(back_keep, back_low)

def segment_ids(places, doc_start, doc_len):
    expanded = places[..., None]
    started = lax.optimization_barrier(jnp.sum((doc_start <= expanded).astype(jnp.int32), axis=-1))
    inside = lax.optimization_barrier(jnp.sum(((doc_start <= expanded) & (expanded < doc_start + doc_len)).astype(jnp.int32), axis=-1))
    segment = 2 * started + 1 - inside
    return jnp.where((places >= 0) & (places < SEQ), segment, -1)

def matmul(left, right):
    return jnp.dot(left, right, precision=precise, preferred_element_type=jnp.float32)

def layer_norm(values, gain_vec, bias_vec):
    centered = values - lax.optimization_barrier(jnp.mean(values, axis=-1, keepdims=True))
    spread = lax.optimization_barrier(jnp.mean(centered * centered, axis=-1, keepdims=True))
    return centered * lax.rsqrt(spread + epsilon) * gain_vec + bias_vec

def attend(queries, key_rows, value_rows, allowed):
    scores = low_back(jnp.einsum('qhe,khe->hqk', queries, key_rows, precision=precise) * 0.125)
    scores = jnp.where(allowed[None], scores, -1e+30)
    highest = lax.optimization_barrier(jnp.max(scores, axis=-1, keepdims=True))
    shares = jnp.exp(scores - highest)
    shares = shares / lax.optimization_barrier(jnp.sum(shares, axis=-1, keepdims=True))
    return jnp.einsum('hqk,khe->qhe', low(shares), value_rows, precision=precise)

def row_layer(weights, row_in, segment):
    w_qkv, w_out, pool_kernel, norm1_gain, norm1_bias, w_up, up_bias, w_down, down_bias, norm2_gain, norm2_bias = weights
    seq_len = row_in.shape[0]
    model_width = row_in.shape[1]
    head_count = model_width // HEAD
    mixed_qkv = low_back(low(matmul(row_in, low(w_qkv))))
    queries = mixed_qkv[:, :model_width]
    keyvals = mixed_qkv[:, model_width:]
    padded = jnp.pad(keyvals, ((2, 2), (0, 0)))
    seg_pad = jnp.pad(segment, (2, 2), constant_values=-1)
    centers = segment[::4]
    pooled = jnp.zeros((seq_len // 4, 2 * model_width), jnp.float32)
    for tap_index in range(5):
        tap_rows = padded[tap_index:tap_index + seq_len].reshape(seq_len // 4, 4, 2 * model_width)[:, 0]
        tap_valid = seg_pad[tap_index:tap_index + seq_len].reshape(seq_len // 4, 4)[:, 0] == centers
        tap_weight = jnp.concatenate([pool_kernel[0, tap_index], pool_kernel[1, tap_index]])
        pooled = pooled + jnp.where(tap_valid[:, None], tap_rows, 0.0) * tap_weight
    pooled = low(pooled)
    block_rows = min(512, seq_len)
    half_win = WIN // 2
    pool_span = PWIN // 2
    pool_reach = pool_span // 4
    key_pad = jnp.pad(keyvals, ((half_win, half_win), (0, 0)))
    seg_key = jnp.pad(segment, (half_win, half_win), constant_values=-1)
    pool_pad = jnp.pad(pooled, ((pool_reach, pool_reach), (0, 0)))
    seg_pool = jnp.pad(centers, (pool_reach, pool_reach), constant_values=-1)

    @jax.checkpoint
    def one_block(first_row):
        q_rows = lax.dynamic_slice_in_dim(queries, first_row, block_rows).reshape(block_rows, head_count, HEAD)
        q_seg = lax.dynamic_slice_in_dim(segment, first_row, block_rows)
        q_place = first_row + jnp.arange(block_rows, dtype=jnp.int32)
        near_count = block_rows + 2 * half_win
        near_rows = lax.dynamic_slice_in_dim(key_pad, first_row, near_count)
        near_seg = lax.dynamic_slice_in_dim(seg_key, first_row, near_count)
        near_place = first_row - half_win + jnp.arange(near_count, dtype=jnp.int32)
        near_gap = near_place[None, :] - q_place[:, None]
        near_ok = (near_seg[None, :] == q_seg[:, None]) & (near_gap >= -half_win) & (near_gap < half_win)
        local_out = attend(q_rows, near_rows[:, :model_width].reshape(near_count, head_count, HEAD), near_rows[:, model_width:].reshape(near_count, head_count, HEAD), near_ok)
        pool_first = first_row // 4
        far_count = block_rows // 4 + 2 * pool_reach
        far_rows = lax.dynamic_slice_in_dim(pool_pad, pool_first, far_count)
        far_seg = lax.dynamic_slice_in_dim(seg_pool, pool_first, far_count)
        far_place = 4 * (pool_first - pool_reach + jnp.arange(far_count, dtype=jnp.int32))
        far_gap = far_place[None, :] - q_place[:, None]
        far_ok = (far_seg[None, :] == q_seg[:, None]) & (far_gap >= -pool_span) & (far_gap < pool_span)
        pool_out = attend(q_rows, far_rows[:, :model_width].reshape(far_count, head_count, HEAD), far_rows[:, model_width:].reshape(far_count, head_count, HEAD), far_ok)
        return (local_out + pool_out).reshape(block_rows, model_width)
    block_starts = jnp.arange(seq_len // block_rows, dtype=jnp.int32) * block_rows
    attended = lax.map(one_block, block_starts).reshape(seq_len, model_width)
    attended = low_back(low(attended))
    branch = low_back(matmul(attended, low(w_out)))
    normed = layer_norm(row_in + branch, norm1_gain, norm1_bias)
    pre_act = low_back(matmul(low(normed), low(w_up)) + up_bias)
    activated = low(jax.nn.gelu(pre_act, approximate=False))
    second = low_back(matmul(activated, low(w_down)) + down_bias)
    return layer_norm(normed + second, norm2_gain, norm2_bias)

def reference(hidden_in, cotangent, w_qkv, w_out, pool_kernel, norm1_gain, norm1_bias, w_up, up_bias, w_down, down_bias, norm2_gain, norm2_bias, doc_lengths, doc_offsets):
    weights = (w_qkv, w_out, pool_kernel, norm1_gain, norm1_bias, w_up, up_bias, w_down, down_bias, norm2_gain, norm2_bias)
    places = jnp.arange(SEQ, dtype=jnp.int32)

    def per_row(running, packed):
        row_in, row_cot, len_row, start_row = packed
        segment = segment_ids(places, start_row, len_row)

        def forward(weight_set, row_values):
            return row_layer(weight_set, row_values, segment)
        result, pullback = jax.vjp(forward, weights, row_in.astype(jnp.float32))
        weight_grads, grad_row = pullback(row_cot.astype(jnp.float32))
        running = jax.tree.map(lambda summed, added: summed + added, running, weight_grads)
        return (running, (result, grad_row))
    zero_grads = jax.tree.map(jnp.zeros_like, weights)
    totals, (row_outs, row_grads) = lax.scan(per_row, zero_grads, (hidden_in, cotangent, doc_lengths, doc_offsets))
    return (row_outs, row_grads, totals[0], totals[1], totals[2], totals[3], totals[4], totals[5], totals[6], totals[7], totals[8], totals[9], totals[10])
```

```python
from functools import partial

import jax
import jax.numpy as jnp
from jax import lax
from jax.sharding import PartitionSpec as P

HEAD = 64
WIN = 128
PWIN = 512


epsilon = 1e-05


def extended(cells, sides, width):
    for axis, dim in sides:
        count = lax.axis_size(axis)
        ends = count - 1
        head = lax.slice_in_dim(cells, 0, width, axis=dim)
        tail = lax.slice_in_dim(cells, cells.shape[dim] - width, cells.shape[dim], axis=dim)
        cells = jnp.concatenate(
            [
                lax.ppermute(tail, axis, [(i, (i + 1) % count) for i in range(ends)]),
                cells,
                lax.ppermute(head, axis, [((i + 1) % count, i) for i in range(ends)]),
            ],
            axis=dim,
        )
    return cells


def segment_ids(places, doc_start, doc_len, seq_len):
    expanded = places[..., None]
    started = jnp.sum((doc_start <= expanded).astype(jnp.int32), axis=-1)
    inside = jnp.sum(
        ((doc_start <= expanded) & (expanded < doc_start + doc_len)).astype(jnp.int32), axis=-1
    )
    segment = 2 * started + 1 - inside
    return jnp.where((places >= 0) & (places < seq_len), segment, -1)


def norm_forward(values, gain_vec, bias_vec):
    centered = values - jnp.mean(values, axis=-1, keepdims=True)
    inv_spread = lax.rsqrt(jnp.mean(centered * centered, axis=-1, keepdims=True) + epsilon)
    unit_vals = centered * inv_spread
    return (unit_vals * gain_vec + bias_vec, unit_vals, inv_spread)


def norm_backward(grad_out, unit_vals, inv_spread, gain_vec):
    grad_unit = grad_out * gain_vec
    grad_values = inv_spread * (
        grad_unit
        - jnp.mean(grad_unit, axis=-1, keepdims=True)
        - unit_vals * jnp.mean(grad_unit * unit_vals, axis=-1, keepdims=True)
    )
    return (grad_values, jnp.sum(grad_out * unit_vals, axis=(0, 1)), jnp.sum(grad_out, axis=(0, 1)))


def scores_of(queries, key_rows, allowed):
    products = (
        jnp.einsum("rqhd,rkhd->rhqk", queries, key_rows, preferred_element_type=jnp.float32) * 0.125
    )
    return jnp.where(allowed[:, None], products, -1e30)


def attend_forward(queries, key_rows, value_rows, allowed):
    scores = scores_of(queries, key_rows, allowed)
    highest = jnp.max(scores, axis=-1, keepdims=True)
    exponent = jnp.exp(scores - highest)
    normalizer = jnp.sum(exponent, axis=-1, keepdims=True)
    shares = (exponent / normalizer).astype(jnp.bfloat16)
    result = jnp.einsum("rhqk,rkhd->rqhd", shares, value_rows, preferred_element_type=jnp.float32)
    return (result, highest + jnp.log(normalizer))


def attend_backward(queries, key_rows, value_rows, allowed, log_total, grad_result):
    scores = scores_of(queries, key_rows, allowed)
    shares = jnp.where(allowed[:, None], jnp.exp(scores - log_total), 0.0)
    grad_shares = jnp.einsum(
        "rqhd,rkhd->rhqk", grad_result, value_rows, preferred_element_type=jnp.float32
    )
    row_inner = jnp.sum(shares * grad_shares, axis=-1, keepdims=True)
    grad_scores = (shares * (grad_shares - row_inner)).astype(jnp.bfloat16)
    grad_query = (
        jnp.einsum("rhqk,rkhd->rqhd", grad_scores, key_rows, preferred_element_type=jnp.float32)
        * 0.125
    )
    grad_key = (
        jnp.einsum("rhqk,rqhd->rkhd", grad_scores, queries, preferred_element_type=jnp.float32)
        * 0.125
    )
    grad_value = jnp.einsum(
        "rhqk,rqhd->rkhd",
        shares.astype(jnp.bfloat16),
        grad_result,
        preferred_element_type=jnp.float32,
    )
    return (grad_query, grad_key, grad_value)


def digit_of(axis, stride, radix):
    return (lax.axis_index(axis) // stride) % radix


def shifted(cells, axis, stride, radix, step):
    pairs = []
    for i in range(lax.axis_size(axis)):
        here = (i // stride) % radix
        pairs.append((i, i + ((here + step) % radix - here) * stride))
    return lax.ppermute(cells, axis, pairs)


def part_of(cells, index):
    return lax.dynamic_index_in_dim(cells, index, 0, keepdims=False)


def scatter_stage(cells, axis, stride, radix):
    mine = digit_of(axis, stride, radix)
    received = [
        shifted(part_of(cells, (mine + k) % radix), axis, stride, radix, k)
        for k in range(1, radix)
    ]
    total = part_of(cells, mine).astype(jnp.float32)
    for piece in received:
        total = total + piece.astype(jnp.float32)
    return total.astype(cells.dtype)


def gather_stage(cells, axis, stride, radix):
    mine = digit_of(axis, stride, radix)
    got = [cells] + [shifted(cells, axis, stride, radix, radix - k) for k in range(1, radix)]
    if radix == 2:
        return jnp.stack(
            [jnp.where(mine == 0, got[0], got[1]), jnp.where(mine == 0, got[1], got[0])]
        )
    return lax.dynamic_slice_in_dim(jnp.stack(got + got), (radix - mine) % radix, radix, 0)


def sum_stage(cells, axis, stride, radix):
    total = cells
    for k in range(1, radix):
        total = total + shifted(cells, axis, stride, radix, k)
    return total


def digits_of(count):
    if count == 8:
        return [(1, 2), (2, 4)]
    digits = []
    stride = 1
    while stride < count:
        digits.append((stride, 2))
        stride *= 2
    return digits


def reduced(cells, dp_first):
    _, rows, columns = cells.shape
    seq_digits = digits_of(lax.axis_size("seq"))
    stride, radix = seq_digits[0]
    cells = cells.reshape(2, 2, rows, columns).transpose(1, 0, 2, 3)
    cells = scatter_stage(cells, "dp", 1, 2)
    if dp_first:
        cells = scatter_stage(cells, "dp", 2, 2).reshape(radix, rows // radix, columns)
        cells = scatter_stage(cells, "seq", stride, radix)
    else:
        cells = cells.reshape(2, radix, rows // radix, columns).transpose(1, 0, 2, 3)
        cells = scatter_stage(cells, "seq", stride, radix)
        cells = scatter_stage(cells, "dp", 2, 2)
    for stride, radix in seq_digits[1:]:
        cells = scatter_stage(
            cells.reshape(radix, cells.shape[0] // radix, columns), "seq", stride, radix
        )
    for stride, radix in reversed(seq_digits):
        cells = gather_stage(cells, "seq", stride, radix).reshape(-1, columns)
    return cells.astype(jnp.float32)


def summed_smalls(parts):
    flat = jnp.concatenate([part.reshape(-1, 768) for part in parts], axis=0)
    for stride, radix in ((1, 2), (2, 2)):
        flat = sum_stage(flat, "dp", stride, radix)
    for stride, radix in digits_of(lax.axis_size("seq")):
        flat = sum_stage(flat, "seq", stride, radix)
    results = []
    first = 0
    for part in parts:
        count = part.size // 768
        results.append(flat[first : first + count].reshape(part.shape))
        first += count
    return results


def placed(block_part, before):
    return jnp.pad(block_part, ((0, 0), (before, 1 - before), (0, 0)))


def local(
    hidden_in,
    cotangent,
    w_qkv,
    w_out,
    pool_kernel,
    norm1_gain,
    norm1_bias,
    w_up,
    up_bias,
    w_down,
    down_bias,
    norm2_gain,
    norm2_bias,
    doc_lengths,
    doc_offsets,
):
    full_qkv, full_out, full_up, full_down = (
        lax.all_gather(w_qkv.astype(jnp.bfloat16), "dp", axis=0, tiled=True),
        lax.all_gather(w_out.astype(jnp.bfloat16), "dp", axis=0, tiled=True),
        lax.all_gather(w_up.astype(jnp.bfloat16), "dp", axis=0, tiled=True),
        lax.all_gather(w_down.astype(jnp.bfloat16), "dp", axis=0, tiled=True),
    )
    row_count, tok_count, model_width = hidden_in.shape
    head_count = model_width // HEAD
    seq_len = tok_count * lax.axis_size("seq")
    anchor = lax.axis_index("seq") * tok_count
    half_win = WIN // 2
    pool_span = PWIN // 2
    pool_reach = pool_span // 4
    pooled_count = tok_count // 4
    doc_start = doc_offsets[:, None, :]
    doc_len = doc_lengths[:, None, :]

    def segments_at(places):
        return segment_ids(
            jnp.broadcast_to(places, (row_count, places.shape[0])), doc_start, doc_len, seq_len
        )

    q_place = anchor + jnp.arange(tok_count, dtype=jnp.int32)
    near_place = anchor - half_win + jnp.arange(tok_count + 2 * half_win, dtype=jnp.int32)
    far_place = 4 * (
        anchor // 4 - pool_reach + jnp.arange(pooled_count + 2 * pool_reach, dtype=jnp.int32)
    )
    q_seg = segments_at(q_place)
    near_seg = segments_at(near_place)
    far_seg = segments_at(far_place)
    near_gap = near_place[None, :] - q_place[:, None]
    far_gap = far_place[None, :] - q_place[:, None]
    near_ok = (
        (near_seg[:, None, :] == q_seg[:, :, None])
        & (near_gap >= -half_win)
        & (near_gap < half_win)
    )
    far_ok = (
        (far_seg[:, None, :] == q_seg[:, :, None]) & (far_gap >= -pool_span) & (far_gap < pool_span)
    )

    def split_heads(tensor):
        return tensor.reshape(tensor.shape[0], tensor.shape[1], head_count, HEAD)

    mixed_qkv = jnp.einsum(
        "rtd,de->rte", hidden_in, full_qkv, preferred_element_type=jnp.float32
    ).astype(jnp.bfloat16)
    queries = mixed_qkv[..., :model_width]
    keyvals = mixed_qkv[..., model_width:]
    near_kv = extended(keyvals, (("seq", 1),), half_win)
    centers = q_seg[:, ::4]
    tap_weights = jnp.concatenate([pool_kernel[0], pool_kernel[1]], axis=-1)
    tap_values = []
    tap_ok = []
    pooled = jnp.zeros((row_count, pooled_count, 2 * model_width), jnp.float32)
    for tap_index in range(5):
        tap_start = half_win - 2 + tap_index
        tap_rows = near_kv[:, tap_start : tap_start + tok_count].reshape(
            row_count, pooled_count, 4, 2 * model_width
        )[:, :, 0]
        seg_taken = near_seg[:, tap_start : tap_start + tok_count].reshape(
            row_count, pooled_count, 4
        )[:, :, 0]
        tap_valid = seg_taken == centers
        tap_values.append(tap_rows)
        tap_ok.append(tap_valid)
        pooled = (
            pooled
            + jnp.where(tap_valid[..., None], tap_rows.astype(jnp.float32), 0.0)
            * tap_weights[tap_index]
        )
    far_kv = extended(pooled.astype(jnp.bfloat16), (("seq", 1),), pool_reach)
    q_heads = split_heads(queries)
    near_k = split_heads(near_kv[..., :model_width])
    near_v = split_heads(near_kv[..., model_width:])
    far_k = split_heads(far_kv[..., :model_width])
    far_v = split_heads(far_kv[..., model_width:])
    near_result, near_log = attend_forward(q_heads, near_k, near_v, near_ok)
    far_result, far_log = attend_forward(q_heads, far_k, far_v, far_ok)
    attended = (
        (near_result + far_result).reshape(row_count, tok_count, model_width).astype(jnp.bfloat16)
    )
    branch = jnp.einsum("rtd,de->rte", attended, full_out, preferred_element_type=jnp.float32)
    normed, unit_one, scale_one = norm_forward(
        hidden_in.astype(jnp.float32) + branch, norm1_gain, norm1_bias
    )
    normed_b = normed.astype(jnp.bfloat16)
    pre_act = (
        jnp.einsum("rtd,df->rtf", normed_b, full_up, preferred_element_type=jnp.float32) + up_bias
    )
    activated, gelu_back = jax.vjp(partial(jax.nn.gelu, approximate=False), pre_act)
    activated_b = activated.astype(jnp.bfloat16)
    second = (
        jnp.einsum("rtf,fd->rtd", activated_b, full_down, preferred_element_type=jnp.float32)
        + down_bias
    )
    block_out, unit_two, scale_two = norm_forward(normed + second, norm2_gain, norm2_bias)
    grad_sum2, grad_gain2, grad_bias2 = norm_backward(
        cotangent.astype(jnp.float32), unit_two, scale_two, norm2_gain
    )
    grad_second = grad_sum2.astype(jnp.bfloat16)
    grad_down_local = jnp.sum(grad_second.astype(jnp.float32), axis=(0, 1))
    term_down = jnp.einsum(
        "rtf,rtd->fd", activated_b, grad_second, preferred_element_type=jnp.float32
    )
    grad_act = jnp.einsum("rtd,fd->rtf", grad_second, full_down, preferred_element_type=jnp.float32)
    (grad_pre,) = gelu_back(grad_act)
    grad_pre_b = grad_pre.astype(jnp.bfloat16)
    grad_up_local = jnp.sum(grad_pre_b.astype(jnp.float32), axis=(0, 1))
    term_up = jnp.einsum("rtd,rtf->df", normed_b, grad_pre_b, preferred_element_type=jnp.float32)
    grad_normed = grad_sum2 + jnp.einsum(
        "rtf,df->rtd", grad_pre_b, full_up, preferred_element_type=jnp.float32
    )
    grad_sum1, grad_gain1, grad_bias1 = norm_backward(grad_normed, unit_one, scale_one, norm1_gain)
    grad_branch = grad_sum1.astype(jnp.bfloat16)
    term_out = jnp.einsum("rtd,rte->de", attended, grad_branch, preferred_element_type=jnp.float32)
    grad_att = jnp.einsum(
        "rte,de->rtd", grad_branch, full_out, preferred_element_type=jnp.float32
    ).astype(jnp.bfloat16)
    grad_att_heads = split_heads(grad_att)
    near_dq, near_dk, near_dv = attend_backward(
        q_heads, near_k, near_v, near_ok, near_log, grad_att_heads
    )
    far_dq, far_dk, far_dv = attend_backward(q_heads, far_k, far_v, far_ok, far_log, grad_att_heads)
    grad_near = jnp.concatenate(
        [near_dk.reshape(row_count, -1, model_width), near_dv.reshape(row_count, -1, model_width)],
        axis=-1,
    )
    grad_far = jnp.concatenate(
        [far_dk.reshape(row_count, -1, model_width), far_dv.reshape(row_count, -1, model_width)],
        axis=-1,
    )
    far_outgoing = jnp.concatenate([grad_far[:, :pool_reach], grad_far[:, -pool_reach:]], axis=1)
    far_incoming = extended(far_outgoing.astype(jnp.bfloat16), (("seq", 1),), pool_reach).astype(
        far_outgoing.dtype
    )
    grad_pooled = (
        grad_far[:, pool_reach : pool_reach + pooled_count]
        + far_incoming[:, :pool_reach]
        + far_incoming[:, -pool_reach:]
    )
    tap_parts = []
    kernel_grad = []
    for tap_index in range(5):
        masked = jnp.where(tap_ok[tap_index][..., None], grad_pooled, 0.0)
        tap_parts.append(masked * tap_weights[tap_index])
        kernel_grad.append(jnp.sum(masked * tap_values[tap_index].astype(jnp.float32), axis=(0, 1)))
    stacked = jnp.stack(
        [
            placed(tap_parts[2], 1),
            placed(tap_parts[3], 1),
            placed(tap_parts[0], 0) + placed(tap_parts[4], 1),
            placed(tap_parts[1], 0),
        ],
        axis=2,
    )
    spread_back = stacked.reshape(row_count, tok_count + 4, 2 * model_width)
    grad_near = grad_near + jnp.pad(spread_back, ((0, 0), (half_win - 4, half_win), (0, 0)))
    pool_grad = jnp.stack(kernel_grad).reshape(5, 2, model_width).transpose(1, 0, 2)
    near_outgoing = jnp.concatenate([grad_near[:, :half_win], grad_near[:, -half_win:]], axis=1)
    near_incoming = extended(near_outgoing.astype(jnp.bfloat16), (("seq", 1),), half_win).astype(
        near_outgoing.dtype
    )
    grad_kv = (
        grad_near[:, half_win : half_win + tok_count]
        + jnp.pad(near_incoming[:, :half_win], ((0, 0), (0, tok_count - half_win), (0, 0)))
        + jnp.pad(near_incoming[:, -half_win:], ((0, 0), (tok_count - half_win, 0), (0, 0)))
    )
    grad_query = (near_dq + far_dq).reshape(row_count, tok_count, model_width)
    grad_mixed = jnp.concatenate([grad_query, grad_kv], axis=-1).astype(jnp.bfloat16)
    term_qkv = jnp.einsum("rtd,rte->de", hidden_in, grad_mixed, preferred_element_type=jnp.float32)
    grad_in = grad_sum1 + jnp.einsum(
        "rte,de->rtd", grad_mixed, full_qkv, preferred_element_type=jnp.float32
    )
    weight_terms = (term_qkv, term_out, term_up, term_down)
    finals = []
    for term, dp_first in zip(weight_terms, (True, True, False, True)):
        term = term.astype(jnp.bfloat16)
        finals.append(reduced(term.reshape(4, term.shape[0] // 4, term.shape[1]), dp_first))
    smalls = summed_smalls(
        (pool_grad, grad_gain1, grad_bias1, grad_up_local, grad_down_local, grad_gain2, grad_bias2)
    )
    return (
        block_out,
        grad_in,
        finals[0],
        finals[1],
        smalls[0],
        smalls[1],
        smalls[2],
        finals[2],
        smalls[3],
        finals[3],
        smalls[4],
        smalls[5],
        smalls[6],
    )


def solution(mesh):
    placed = (
        P("dp", "seq", None),
        P("dp", "seq", None),
        P("dp", None),
        P("dp", None),
        P(),
        P(),
        P(),
        P("dp", None),
        P(),
        P("dp", None),
        P(),
        P(),
        P(),
        P("dp", None),
        P("dp", None),
    )
    return jax.shard_map(
        local,
        mesh=mesh,
        in_specs=placed,
        out_specs=(
            P("dp", "seq", None),
            P("dp", "seq", None),
            P("dp", None),
            P("dp", None),
            P(),
            P(),
            P(),
            P("dp", None),
            P(),
            P("dp", None),
            P(),
            P(),
            P(),
        ),
        check_vma=False,
    )
```

```python
from functools import partial

import jax
import jax.numpy as jnp
from jax import lax
from jax.experimental import pallas as pl
from jax.experimental.pallas import tpu as pltpu
from jax.sharding import PartitionSpec as P

HEAD = 64
WIN = 128
PWIN = 512
LANES = 128
GROUP = 256
BLOCK = 128
PAD = 16
F32 = jnp.float32
BF16 = jnp.bfloat16

SMALL_COST = pl.CostEstimate(flops=10**11, bytes_accessed=1, transcendentals=0)

epsilon = 1e-05


def digit_of(axis, stride, radix):
    return (lax.axis_index(axis) // stride) % radix


def shifted(cells, axis, stride, radix, step):
    pairs = []
    for i in range(lax.axis_size(axis)):
        here = (i // stride) % radix
        pairs.append((i, i + ((here + step) % radix - here) * stride))
    return lax.ppermute(cells, axis, pairs)


def moved(cells, step):
    count = lax.axis_size("seq")
    pairs = [(i, i + step) for i in range(count) if 0 <= i + step < count]
    return lax.ppermute(cells, "seq", pairs)


def after(cells, *earlier):
    return lax.optimization_barrier((cells, *earlier))[0]


def gathered(shard):
    return shard, shifted(shard, "dp", 1, 2, 1), shifted(shard, "dp", 2, 2, 1)


def with_last(pieces, *earlier):
    partner = after(pieces[2], *earlier) if earlier else pieces[2]
    return *pieces, shifted(partner, "dp", 1, 2, 1)


def piece_owners():
    mine = lax.axis_index("dp")
    turn = 1 - 2 * lax.rem(mine, 2)
    partner = lax.rem(mine + 2, 4)
    return mine, mine + turn, partner, partner + turn


class Order:
    def __init__(self, last):
        self.last = last

    def __call__(self, step, cells, *rest, **options):
        out = step(after(cells, self.last), *rest, **options)
        self.last = out[0]
        return out


def bit_of(name):
    if name in "cy":
        return "dp", 1 << "cy".index(name)
    return "seq", 1 << "xlhijk".index(name)


def mine_of(name):
    return digit_of(*bit_of(name), 2)


def swapped(cells, name):
    axis, stride = bit_of(name)
    return shifted(cells, axis, stride, 2, 1)


def added(kept, received):
    return (kept.astype(F32) + received.astype(F32)).astype(BF16)


def split(kept, received, dim, name):
    mine = mine_of(name)

    def part(index):
        return added(
            lax.dynamic_index_in_dim(kept, index, dim, keepdims=False),
            lax.dynamic_index_in_dim(received, index, dim, keepdims=False),
        )

    return part(1 - mine), part(mine)


def summed(kept, received):
    return (added(kept, received),)


def joined(own, received, dim, name, dtype=BF16):
    first = mine_of(name) == 0
    cells = jnp.stack(
        [jnp.where(first, own, received), jnp.where(first, received, own)], axis=dim
    )
    return (cells.astype(dtype),)


def input_sum_kernel(own, left, right, last, out):
    tokens = own.shape[1]
    out[...] = own[...] + left[...].astype(F32) + right[...].astype(F32)
    out[:, tokens - PAD :] += last[...].astype(F32)


def input_sum(own, left, right, last):
    rows, tokens, width = own.shape
    block = pl.BlockSpec((1, tokens, width), lambda i: (i, 0, 0))
    return pl.pallas_call(
        input_sum_kernel,
        grid=(rows,),
        in_specs=[block] * 3 + [pl.BlockSpec((1, PAD, width), lambda i: (i, 0, 0))],
        out_specs=[block],
        out_shape=[jax.ShapeDtypeStruct(own.shape, F32)],
        compiler_params=pltpu.CompilerParams(vmem_limit_bytes=60 * 2**20),
        cost_estimate=SMALL_COST,
        name="input_sum",
    )(own, left, right, last)


def dot_nn(a, b):
    return jnp.dot(a, b, preferred_element_type=F32)


def dot_nt(a, b):
    return lax.dot_general(a, b, (((1,), (1,)), ((), ())), preferred_element_type=F32)


def dot_tn(a, b):
    return lax.dot_general(a, b, (((0,), (0,)), ((), ())), preferred_element_type=F32)


def segment_of(place, starts, lengths, seq_len):
    started = jnp.zeros(place.shape, jnp.int32)
    inside = jnp.zeros(place.shape, jnp.int32)
    for start, length in zip(starts, lengths):
        begun = place >= start
        started = started + jnp.where(begun, 1, 0)
        inside = inside + jnp.where(begun & (place < start + length), 1, 0)
    return jnp.where((place >= 0) & (place < seq_len), 2 * started + 1 - inside, -1)


def iota_of(shape, dim):
    return lax.broadcasted_iota(jnp.int32, shape, dim)


def allowed_bias(q_place, k_place, segment, reach):
    gap = k_place - q_place
    allowed = (segment(q_place) == segment(k_place)) & (gap >= -reach) & (gap < reach)
    return jnp.where(allowed, 0.0, -1e30)


def head_pair(block):
    first = iota_of(block.shape, 1) < HEAD
    zero = jnp.zeros(block.shape, block.dtype)
    return jnp.concatenate([jnp.where(first, block, zero), jnp.where(first, zero, block)], axis=0)


def join_pair(pair):
    rows = pair.shape[0] // 2
    first = iota_of((rows, LANES), 1) < HEAD
    return jnp.where(first, pair[:rows], pair[rows:])


def relative_rows(index, rows):
    core = lax.rem(lax.axis_index("dp"), 2)
    same = 1 - (core + index % 2 - 2 * core * (index % 2))
    return pl.ds(pl.multiple_of((2 * same + index // 2) * rows, 16), rows)


def row_docs(starts_ref, lengths_ref, row, slots):
    return (
        [starts_ref[row, j] for j in range(slots)],
        [lengths_ref[row, j] for j in range(slots)],
    )


def copy_all(copies):
    for copy in copies:
        copy.start()
    for copy in copies:
        copy.wait()


def token_copies(pieces, scratch, sems, rows, tokens):
    copies = []
    extent = PAD + 3 * tokens
    firsts = (0, PAD, PAD + tokens, PAD + 2 * tokens)
    for row in range(rows):
        for k, (piece, first) in enumerate(zip(pieces, firsts)):
            count = PAD if k == 0 else tokens
            copies.append(
                pltpu.make_async_copy(
                    piece.at[row],
                    scratch.at[pl.ds(row * extent + first, count)],
                    sems.at[row * 4 + k],
                )
            )
    return copies


def weight_copies(pieces, scratch, sems, rows):
    return [
        pltpu.make_async_copy(
            piece, scratch.at[pl.ds(pl.multiple_of(index * rows, 16), rows)], sems.at[k]
        )
        for k, (piece, index) in enumerate(zip(pieces, piece_owners()))
    ]


def tap_mask(row, tap, reach, pooled, tokens, starts_ref, lengths_ref, slots, seq_len):
    anchor = lax.axis_index("seq") * tokens
    center = anchor - 4 * reach + 4 * iota_of((pooled, LANES), 0)
    segment = partial(
        segment_of,
        seq_len=seq_len,
        **dict(zip(("starts", "lengths"), row_docs(starts_ref, lengths_ref, row, slots))),
    )
    return jnp.where(segment(center + (tap - 2)) == segment(center), 1.0, 0.0)


def forward_kernel(
    sizes,
    starts_ref,
    lengths_ref,
    x_ll,
    x_l,
    x_own,
    x_r,
    w0,
    w1,
    w2,
    w3,
    pool_ref,
    q_out,
    k_out,
    v_out,
    pk_out,
    pv_out,
    att_out,
    xs,
    ws,
    flat,
    near_bias,
    far_bias,
    taps_ok,
    x_sems,
    w_sems,
):
    rows, tokens, width, seq_len, slots = sizes
    step = pl.program_id(0)
    extent = PAD + 3 * tokens
    half_win = WIN // 2
    reach = PWIN // 8
    pooled = tokens // 4 + 2 * reach
    blocks = tokens // BLOCK
    span = BLOCK + 2 * half_win
    anchor = lax.axis_index("seq") * tokens

    @pl.when(step == 0)
    def _():
        copies = token_copies((x_ll, x_l, x_own, x_r), xs, x_sems, rows, tokens)
        copies += weight_copies((w0, w1, w2, w3), ws, w_sems, width // 4)
        for copy in copies:
            copy.start()
        for row in range(rows):
            starts, lengths = row_docs(starts_ref, lengths_ref, row, slots)
            segment = partial(segment_of, starts=starts, lengths=lengths, seq_len=seq_len)
            for block in range(blocks):
                q_place = anchor + block * BLOCK + iota_of((BLOCK, 1), 0)
                near_place = anchor + block * BLOCK - half_win + iota_of((1, span), 1)
                far_place = anchor - 4 * reach + 4 * iota_of((1, pooled), 1)
                near_bias[row, block] = allowed_bias(q_place, near_place, segment, half_win)
                far_bias[row, block] = allowed_bias(q_place, far_place, segment, 4 * reach)
            for tap in range(5):
                taps_ok[row, tap] = tap_mask(
                    row, tap, reach, pooled, tokens, starts_ref, lengths_ref, slots, seq_len
                )
        for copy in copies:
            copy.wait()

    def columns(part):
        return pl.ds(pl.multiple_of(part * width + step * GROUP, LANES), GROUP)

    x_all = xs[...]
    for row in range(rows):
        own = xs[pl.ds(row * extent + PAD + tokens, tokens)]
        q_out[row] = dot_nn(own, ws[:, columns(0)]).astype(BF16)
    for part, out, pooled_out in ((1, k_out, pk_out), (2, v_out, pv_out)):
        cells = dot_nn(x_all, ws[:, columns(part)]).astype(BF16)
        out[...] = cells.reshape(rows, extent, GROUP)
        for half in range(GROUP // LANES):
            lanes = pl.ds(half * LANES, LANES)
            flat[half] = cells[:, half * LANES : (half + 1) * LANES].astype(F32)
            for row in range(rows):
                total = jnp.zeros((pooled, LANES), F32)
                for tap in range(5):
                    first = row * extent + PAD - 2 + tap
                    tap_rows = flat[half, pl.ds(first, pooled, stride=4)]
                    total = total + tap_rows * taps_ok[row, tap] * pool_ref[part - 1, tap, lanes]
                pooled_out[row, :, lanes] = total.astype(BF16)
    for row in range(rows):
        for half in range(GROUP // LANES):
            lanes = pl.ds(half * LANES, LANES)
            for block in range(blocks):
                queries = q_out[row, pl.ds(block * BLOCK, BLOCK), lanes] * 0.125
                window = pl.ds(PAD + tokens + block * BLOCK - half_win, span)
                keys = jnp.concatenate([k_out[row, window, lanes], pk_out[row, :, lanes]], axis=0)
                values = jnp.concatenate([v_out[row, window, lanes], pv_out[row, :, lanes]], axis=0)
                scores = dot_nt(head_pair(queries.astype(BF16)), keys)
                scores = scores.reshape(2, BLOCK, span + pooled)
                shares = []
                for part, bias in (
                    (scores[..., :span], near_bias[row, block]),
                    (scores[..., span:], far_bias[row, block]),
                ):
                    part = part + bias
                    exponent = jnp.exp(part - jnp.max(part, axis=-1, keepdims=True))
                    normalizer = jnp.sum(exponent, axis=-1, keepdims=True)
                    shares.append((exponent * (1.0 / normalizer)).astype(BF16))
                shares = jnp.concatenate(shares, axis=-1).reshape(2 * BLOCK, span + pooled)
                result = join_pair(dot_nn(shares, values))
                att_out[row, pl.ds(block * BLOCK, BLOCK), lanes] = result.astype(BF16)


def whole(memory_space):
    return pl.BlockSpec(memory_space=memory_space)


def group_block(*lead):
    zeros = (0,) * len(lead)
    return pl.BlockSpec(lead + (GROUP,), lambda g: zeros + (g,))


def attention_forward(starts, lengths, tokens_in, w_pieces, pool_kernel, seq_len):
    rows, tokens, width = tokens_in[2].shape
    extent = PAD + 3 * tokens
    pooled = tokens // 4 + PWIN // 4
    blocks = tokens // BLOCK
    span = BLOCK + WIN
    slots = starts.shape[1]
    return pl.pallas_call(
        partial(forward_kernel, (rows, tokens, width, seq_len, slots)),
        grid=(width // GROUP,),
        in_specs=[whole(pltpu.SMEM)] * 2 + [whole(pl.ANY)] * 8 + [group_block(2, 5)],
        out_specs=[
            group_block(rows, tokens),
            group_block(rows, extent),
            group_block(rows, extent),
            group_block(rows, pooled),
            group_block(rows, pooled),
            group_block(rows, tokens),
        ],
        out_shape=[
            jax.ShapeDtypeStruct((rows, count, width), BF16)
            for count in (tokens, extent, extent, pooled, pooled, tokens)
        ],
        scratch_shapes=[
            pltpu.VMEM((rows * extent, width), BF16),
            pltpu.VMEM((width, 3 * width), BF16),
            pltpu.VMEM((GROUP // LANES, rows * extent, LANES), F32),
            pltpu.VMEM((rows, blocks, BLOCK, span), F32),
            pltpu.VMEM((rows, blocks, BLOCK, pooled), F32),
            pltpu.VMEM((rows, 5, pooled, LANES), F32),
            pltpu.SemaphoreType.DMA((4 * rows,)),
            pltpu.SemaphoreType.DMA((4,)),
        ],
        compiler_params=pltpu.CompilerParams(vmem_limit_bytes=60 * 2**20),
        cost_estimate=SMALL_COST,
        name="attention_forward",
    )(starts, lengths, *tokens_in, *w_pieces, pool_kernel)


def backward_kernel(
    sizes,
    starts_ref,
    lengths_ref,
    x_ll,
    x_l,
    x_own,
    x_r,
    pool_ref,
    q_ref,
    k_ref,
    v_ref,
    pk_ref,
    pv_ref,
    grad_ref,
    dw_sent_in,
    dw_kept_in,
    dw_sent,
    dw_kept,
    dpool_out,
    dq_out,
    dkv_out,
    xs,
    x_turned,
    own_turned,
    flat,
    grad_flat,
    grad_pooled,
    near_bias,
    far_bias,
    taps_ok,
    dw,
    x_sems,
    dw_sems,
):
    first_group, rows, tokens, width, seq_len, slots = sizes
    quarter = width // 4
    step = pl.program_id(0)
    extent = PAD + 3 * tokens
    half_win = WIN // 2
    reach = PWIN // 8
    pooled = tokens // 4 + 2 * reach
    blocks = tokens // BLOCK
    span = BLOCK + 2 * half_win
    anchor = lax.axis_index("seq") * tokens

    @pl.when(step == 0)
    def _():
        copies = token_copies((x_ll, x_l, x_own, x_r), xs, x_sems, rows, tokens)
        for copy in copies:
            copy.start()
        for row in range(rows):
            starts, lengths = row_docs(starts_ref, lengths_ref, row, slots)
            segment = partial(segment_of, starts=starts, lengths=lengths, seq_len=seq_len)
            for block in range(blocks):
                q_place = anchor + block * BLOCK + iota_of((1, BLOCK), 1)
                near_place = anchor + block * BLOCK - half_win + iota_of((span, 1), 0)
                far_place = anchor - 4 * reach + 4 * iota_of((pooled, 1), 0)
                near = allowed_bias(q_place, near_place, segment, half_win)
                far = allowed_bias(q_place, far_place, segment, 4 * reach)
                near_bias[row, block] = jnp.concatenate([near, near], axis=1)
                far_bias[row, block] = jnp.concatenate([far, far], axis=1)
            for tap in range(5):
                taps_ok[row, tap] = tap_mask(
                    row, tap, reach, pooled, tokens, starts_ref, lengths_ref, slots, seq_len
                )
        for copy in copies:
            copy.wait()
        for index in range(4):
            features = pl.ds(index * quarter, quarter)
            place = relative_rows(index, quarter)
            x_turned[place] = xs[:, features].T
            for row in range(rows):
                own_turned[place, pl.ds(row * tokens, tokens)] = xs[
                    pl.ds(row * extent + PAD + tokens, tokens), features
                ].T

    grad_flat[...] = jnp.zeros(grad_flat.shape, F32)
    grad_pooled[...] = jnp.zeros(grad_pooled.shape, F32)
    for row in range(rows):
        for half in range(GROUP // LANES):
            lanes = pl.ds(half * LANES, LANES)
            for block in range(blocks):
                queries = q_ref[row, pl.ds(block * BLOCK, BLOCK), lanes] * 0.125
                queries = head_pair(queries.astype(BF16))
                grads = head_pair(grad_ref[row, pl.ds(block * BLOCK, BLOCK), lanes])
                window_first = PAD + tokens + block * BLOCK - half_win
                window = pl.ds(window_first, span)
                keys = jnp.concatenate([k_ref[row, window, lanes], pk_ref[row, :, lanes]], axis=0)
                values = jnp.concatenate([v_ref[row, window, lanes], pv_ref[row, :, lanes]], axis=0)
                scores = dot_nt(keys, queries)
                grad_shares = dot_nt(values, grads)
                shares_b = []
                grad_scores = []
                for part, bias, grad_part in (
                    (scores[:span], near_bias[row, block], grad_shares[:span]),
                    (scores[span:], far_bias[row, block], grad_shares[span:]),
                ):
                    part = part + bias
                    exponent = jnp.exp(part - jnp.max(part, axis=0, keepdims=True))
                    shares = exponent * (1.0 / jnp.sum(exponent, axis=0, keepdims=True))
                    inner = jnp.sum(shares * grad_part, axis=0, keepdims=True)
                    shares_b.append(shares.astype(BF16))
                    grad_scores.append((shares * (grad_part - inner)).astype(BF16))
                shares_b = jnp.concatenate(shares_b, axis=0)
                grad_scores = jnp.concatenate(grad_scores, axis=0)
                grad_queries = join_pair(dot_tn(grad_scores, keys)) * 0.125
                dq_out[pl.ds(row * tokens + block * BLOCK, BLOCK), lanes] = grad_queries.astype(
                    BF16
                )
                for index, grad_rows in (
                    (0, dot_nn(grad_scores, queries)),
                    (1, dot_nn(shares_b, grads)),
                ):
                    near_rows = pl.ds(row * extent + window_first, span)
                    grad_flat[index, half, near_rows] += grad_rows[:span]
                    far_rows = pl.ds(row * pooled, pooled)
                    grad_pooled[index, far_rows, lanes] += grad_rows[span:]

    for index, cells in ((0, k_ref), (1, v_ref)):
        for half in range(GROUP // LANES):
            lanes = pl.ds(half * LANES, LANES)
            flat[...] = cells[:, :, lanes].reshape(rows * extent, LANES).astype(F32)
            for tap in range(5):
                total = jnp.zeros((1, LANES), F32)
                for row in range(rows):
                    places = pl.ds(row * extent + PAD - 2 + tap, pooled, stride=4)
                    grads = grad_pooled[index, pl.ds(row * pooled, pooled), lanes]
                    grads = grads * taps_ok[row, tap]
                    total = total + jnp.sum(grads * flat[places], axis=0, keepdims=True)
                    grad_flat[index, half, places] = (
                        grad_flat[index, half, places] + grads * pool_ref[index, tap, lanes]
                    )
                dpool_out[index, pl.ds(tap, 1), lanes] = total

    slot = lax.rem(step, 2)

    def dw_copies(slot, group):
        columns = pl.ds(pl.multiple_of(group * GROUP, LANES), GROUP)
        return [
            pltpu.make_async_copy(
                dw.at[slot, k], out.at[:, pl.ds(0, 3), :, columns], dw_sems.at[slot, k]
            )
            for k, out in enumerate((dw_sent, dw_kept))
        ]

    @pl.when(step >= 2)
    def _():
        for copy in dw_copies(slot, first_group + step - 2):
            copy.wait()

    def put(index, cells):
        dw[slot, :, :, index] = cells.astype(BF16).reshape(2, 2, quarter, GROUP)

    put(0, dot_nn(own_turned[...], dq_out[...]))
    for index in range(2):
        cells = jnp.concatenate(
            [grad_flat[index, half] for half in range(GROUP // LANES)], axis=1
        ).astype(BF16)
        dkv_out[index] = cells
        put(1 + index, dot_nn(x_turned[...], cells))
    for copy in dw_copies(slot, first_group + step):
        copy.start()

    @pl.when(step == pl.num_programs(0) - 1)
    def _():
        for copy in dw_copies(slot, first_group + step):
            copy.wait()

    @pl.when((step == pl.num_programs(0) - 1) & (step >= 1))
    def _():
        for copy in dw_copies(1 - slot, first_group + step - 1):
            copy.wait()


def attention_backward(
    grad_att, dw_sent, dw_kept, starts, lengths, tokens_in, pool_kernel, saved, seq_len, groups
):
    rows, tokens, width = tokens_in[2].shape
    extent = PAD + 3 * tokens
    pooled = tokens // 4 + PWIN // 4
    blocks = tokens // BLOCK
    span = BLOCK + WIN
    slots = starts.shape[1]
    quarter = width // 4
    first, count = groups
    columns = count * GROUP

    def read(*lead):
        zeros = (0,) * len(lead)
        return pl.BlockSpec(lead + (GROUP,), lambda g: zeros + (g + first,))

    return pl.pallas_call(
        partial(backward_kernel, (first, rows, tokens, width, seq_len, slots)),
        grid=(count,),
        in_specs=[whole(pltpu.SMEM)] * 2
        + [whole(pl.ANY)] * 4
        + [read(2, 5)]
        + [read(rows, size) for size in (tokens, extent, extent, pooled, pooled, tokens)]
        + [whole(pl.ANY)] * 2,
        out_specs=[
            whole(pl.ANY),
            whole(pl.ANY),
            group_block(2, 5),
            group_block(rows * tokens),
            group_block(2, rows * extent),
        ],
        out_shape=[
            jax.ShapeDtypeStruct(dw_sent.shape, BF16),
            jax.ShapeDtypeStruct(dw_kept.shape, BF16),
            jax.ShapeDtypeStruct((2, 5, columns), F32),
            jax.ShapeDtypeStruct((rows * tokens, columns), BF16),
            jax.ShapeDtypeStruct((2, rows * extent, columns), BF16),
        ],
        scratch_shapes=[
            pltpu.VMEM((rows * extent, width), BF16),
            pltpu.VMEM((width, rows * extent), BF16),
            pltpu.VMEM((width, rows * tokens), BF16),
            pltpu.VMEM((rows * extent, LANES), F32),
            pltpu.VMEM((2, GROUP // LANES, rows * extent, LANES), F32),
            pltpu.VMEM((2, rows * pooled, GROUP), F32),
            pltpu.VMEM((rows, blocks, span, 2 * BLOCK), F32),
            pltpu.VMEM((rows, blocks, pooled, 2 * BLOCK), F32),
            pltpu.VMEM((rows, 5, pooled, LANES), F32),
            pltpu.VMEM((2, 2, 2, 3, quarter, GROUP), BF16),
            pltpu.SemaphoreType.DMA((4 * rows,)),
            pltpu.SemaphoreType.DMA((2, 2)),
        ],
        input_output_aliases={13: 0, 14: 1},
        compiler_params=pltpu.CompilerParams(vmem_limit_bytes=60 * 2**20),
        cost_estimate=SMALL_COST,
        name="attention_backward",
    )(starts, lengths, *tokens_in, pool_kernel, *saved, grad_att, dw_sent, dw_kept)


def input_kernel(sizes, w0, w1, w2, w3, *refs):
    parts, rows, tokens, width = sizes
    grad_q = refs[:parts]
    grad_kv = refs[parts : 2 * parts]
    sum1_ref, dx_own, dx_ll, dx_l, dx_r, ws, sems = refs[2 * parts :]
    extent = PAD + 3 * tokens
    copy_all(weight_copies((w0, w1, w2, w3), ws, sems, width // 4))

    def term(row, first, count, with_queries):
        total = None
        column = 0
        for queries, keyvals in zip(grad_q, grad_kv):
            size = queries.shape[1]
            places = pl.ds(row * extent + first, count)
            terms = [
                (keyvals[index, places], ws[:, pl.ds((1 + index) * width + column, size)])
                for index in range(2)
            ]
            if with_queries:
                terms.append((queries[pl.ds(row * tokens, tokens)], ws[:, pl.ds(column, size)]))
            for grads, weights in terms:
                part = dot_nt(grads, weights)
                total = part if total is None else total + part
            column += size
        return total

    for row in range(rows):
        ahead = term(row, 0, PAD + tokens, False).astype(BF16)
        dx_ll[row] = ahead[:PAD]
        dx_l[row] = ahead[PAD:]
        dx_own[row] = term(row, PAD + tokens, tokens, True) + sum1_ref[row]
        dx_r[row] = term(row, PAD + 2 * tokens, tokens, False).astype(BF16)


def input_gradient(grad_sum1, w_pieces, grad_q, grad_kv):
    rows, tokens, width = grad_sum1.shape
    return pl.pallas_call(
        partial(input_kernel, (len(grad_q), rows, tokens, width)),
        in_specs=[whole(pl.ANY)] * 4 + [whole(pltpu.VMEM)] * (2 * len(grad_q) + 1),
        out_specs=[whole(pltpu.VMEM)] * 4,
        out_shape=[
            jax.ShapeDtypeStruct((rows, tokens, width), F32),
            jax.ShapeDtypeStruct((rows, PAD, width), BF16),
            jax.ShapeDtypeStruct((rows, tokens, width), BF16),
            jax.ShapeDtypeStruct((rows, tokens, width), BF16),
        ],
        scratch_shapes=[pltpu.VMEM((width, 3 * width), BF16), pltpu.SemaphoreType.DMA((4,))],
        compiler_params=pltpu.CompilerParams(vmem_limit_bytes=60 * 2**20),
        cost_estimate=SMALL_COST,
        name="input_gradient",
    )(*w_pieces, *grad_q, *grad_kv, grad_sum1)


def normalized(values):
    centered = values - jnp.mean(values, axis=-1, keepdims=True)
    scale = lax.rsqrt(jnp.mean(centered * centered, axis=-1, keepdims=True) + epsilon)
    return centered * scale, scale


def norm_back(grad_unit, unit, scale):
    return scale * (
        grad_unit
        - jnp.mean(grad_unit, axis=-1, keepdims=True)
        - unit * jnp.mean(grad_unit * unit, axis=-1, keepdims=True)
    )


def column_sum(cells):
    return jnp.sum(cells, axis=0, keepdims=True)


def token_kernel(
    att_ref,
    x_ref,
    cot_ref,
    w0,
    w1,
    w2,
    w3,
    gain1_ref,
    bias1_ref,
    up_bias_ref,
    down_bias_ref,
    gain2_ref,
    bias2_ref,
    out_ref,
    grad_att_out,
    sum1_out,
    down_sent,
    down_kept,
    up_sent,
    up_kept,
    qkv_sent,
    qkv_kept,
    smalls_out,
    w_out,
    w_up,
    w_down,
    unit1,
    scale1,
    normed_b,
    act,
    slope,
    second,
    turned,
    dw_down,
    dw_up,
    dw_out,
    sems,
    dw_sems,
):
    width = att_ref.shape[1]
    count = w_up.shape[0]
    quarter = width // 4
    core = lax.rem(lax.axis_index("dp"), 2)

    def turn(cells):
        for index in range(4):
            turned[relative_rows(index, quarter)] = cells[:, pl.ds(index * quarter, quarter)].T

    out_copies = []

    def send(source, target):
        copy = pltpu.make_async_copy(source, target, dw_sems.at[len(out_copies)])
        copy.start()
        out_copies.append(copy)

    copies = []
    for piece, index in zip((w0, w1, w2, w3), piece_owners()):
        for column in range(1 + count + 4):
            if column == 0:
                target, base = w_out, index * quarter
            elif column <= count:
                target, base = w_up.at[column - 1], index * quarter
            else:
                target, base = w_down.at[index], (column - 1 - count) * quarter
            copies.append(
                pltpu.make_async_copy(
                    piece.at[:, pl.ds(column * width, width)],
                    target.at[pl.ds(pl.multiple_of(base, 16), quarter)],
                    sems.at[len(copies)],
                )
            )
    copy_all(copies)

    first_sum = x_ref[...].astype(F32) + dot_nn(att_ref[...], w_out[...])
    unit, scale = normalized(first_sum)
    unit1[...] = unit
    scale1[...] = scale
    normed = unit * gain1_ref[...] + bias1_ref[...]
    normed_b[...] = normed.astype(BF16)
    second[...] = normed + down_bias_ref[...]
    for block in range(count):
        pre = dot_nn(normed_b[...], w_up[block]) + up_bias_ref[pl.ds(block, 1)]
        below = 0.5 * (1.0 + lax.erf(pre * (0.5**0.5)))
        act[block] = (pre * below).astype(BF16)
        slope[block] = below + pre * jnp.exp(-0.5 * pre * pre) * 0.3989422804014327
        second[...] += dot_nn(act[block], w_down[block])

    unit, scale = normalized(second[...])
    out_ref[...] = unit * gain2_ref[...] + bias2_ref[...]
    cot = cot_ref[...].astype(F32)
    smalls_out[pl.ds(3, 1)] = column_sum(cot * unit)
    smalls_out[pl.ds(4, 1)] = column_sum(cot)
    grad_sum2 = norm_back(cot * gain2_ref[...], unit, scale)
    second[...] = grad_sum2
    grad_second = grad_sum2.astype(BF16)
    smalls_out[pl.ds(2, 1)] = column_sum(grad_second.astype(F32))
    turn(normed_b)
    for y in range(2):
        for same, target in ((0, down_sent), (1, down_kept)):
            block = 2 * y + same * core + (1 - same) * (1 - core)
            dw_down[same, y] = dot_tn(act[block], grad_second).astype(BF16)
            send(dw_down.at[same, y], target.at[y])
    for block in range(count):
        grad_pre = (dot_nt(grad_second, w_down[block]) * slope[block]).astype(BF16)
        smalls_out[pl.ds(5 + block, 1)] = column_sum(grad_pre.astype(F32))
        dw_up[block] = dot_nn(turned[...], grad_pre).astype(BF16)
        for same, target in ((0, up_sent), (1, up_kept)):
            for y in range(2):
                send(
                    dw_up.at[block, pl.ds((2 * same + y) * quarter, quarter)],
                    target.at[y, pl.ds(block * quarter, quarter)],
                )
        second[...] += dot_nt(grad_pre, w_up[block])

    grad_normed = second[...]
    unit = unit1[...]
    smalls_out[pl.ds(0, 1)] = column_sum(grad_normed * unit)
    smalls_out[pl.ds(1, 1)] = column_sum(grad_normed)
    grad_sum1 = norm_back(grad_normed * gain1_ref[...], unit, scale1[...])
    sum1_out[...] = grad_sum1
    grad_branch = grad_sum1.astype(BF16)
    turn(att_ref)
    dw_out[...] = dot_nn(turned[...], grad_branch).astype(BF16)
    for same, target in ((0, qkv_sent), (1, qkv_kept)):
        for y in range(2):
            send(dw_out.at[pl.ds((2 * same + y) * quarter, quarter)], target.at[y, 3])
    grad_att_out[...] = dot_nt(grad_branch, w_out[...]).astype(BF16)
    for copy in out_copies:
        copy.wait()


def token_part(attended, hidden_in, cotangent, w_pieces, vectors):
    rows, tokens, width = hidden_in.shape
    total = rows * tokens
    gain1, bias1, up_bias, down_bias, gain2, bias2 = vectors
    hidden = up_bias.shape[0]
    count = hidden // width
    return pl.pallas_call(
        token_kernel,
        in_specs=[whole(pltpu.VMEM)] * 3 + [whole(pl.ANY)] * 4 + [whole(pltpu.VMEM)] * 6,
        out_specs=[whole(pltpu.VMEM)] * 3 + [whole(pl.ANY)] * 6 + [whole(pltpu.VMEM)],
        out_shape=[
            jax.ShapeDtypeStruct((total, width), F32),
            jax.ShapeDtypeStruct((total, width), BF16),
            jax.ShapeDtypeStruct((total, width), F32),
        ]
        + [jax.ShapeDtypeStruct((2, width, width), BF16)] * 4
        + [jax.ShapeDtypeStruct((2, 4, width // 4, width), BF16)] * 2
        + [jax.ShapeDtypeStruct((5 + count, width), F32)],
        scratch_shapes=[
            pltpu.VMEM((width, width), BF16),
            pltpu.VMEM((count, width, width), BF16),
            pltpu.VMEM((count, width, width), BF16),
            pltpu.VMEM((total, width), F32),
            pltpu.VMEM((total, 1), F32),
            pltpu.VMEM((total, width), BF16),
            pltpu.VMEM((count, total, width), BF16),
            pltpu.VMEM((count, total, width), F32),
            pltpu.VMEM((total, width), F32),
            pltpu.VMEM((width, total), BF16),
            pltpu.VMEM((2, 2, width, width), BF16),
            pltpu.VMEM((count, width, width), BF16),
            pltpu.VMEM((width, width), BF16),
            pltpu.SemaphoreType.DMA((4 * (5 + count),)),
            pltpu.SemaphoreType.DMA((8 + 4 * count,)),
        ],
        compiler_params=pltpu.CompilerParams(vmem_limit_bytes=60 * 2**20),
        cost_estimate=SMALL_COST,
        name="token_part",
    )(
        attended.reshape(total, width),
        hidden_in.reshape(total, width),
        cotangent.reshape(total, width),
        *w_pieces,
        gain1.reshape(1, width),
        bias1.reshape(1, width),
        up_bias.reshape(count, width),
        down_bias.reshape(1, width),
        gain2.reshape(1, width),
        bias2.reshape(1, width),
    )


def local(
    hidden_in,
    cotangent,
    w_qkv,
    w_out,
    pool_kernel,
    norm1_gain,
    norm1_bias,
    w_up,
    up_bias,
    w_down,
    down_bias,
    norm2_gain,
    norm2_bias,
    doc_lengths,
    doc_offsets,
):
    rows, tokens, width = hidden_in.shape
    quarter = width // 4
    hidden = up_bias.shape[0]
    seq_len = tokens * lax.axis_size("seq")
    tokens_in = (
        moved(hidden_in[:, tokens - PAD :], 2),
        moved(hidden_in, 1),
        hidden_in,
    )
    qkv_pieces = with_last(gathered(w_qkv.astype(BF16)))
    tokens_in += (moved(after(hidden_in, tokens_in[1]), -1),)
    rest = jnp.concatenate(
        [w_out, w_up, w_down.reshape(4, quarter, width).transpose(1, 0, 2).reshape(quarter, hidden)],
        axis=1,
    )
    rest_pieces = gathered(
        after(rest.astype(BF16), qkv_pieces[2], tokens_in[1])
    )
    *saved, attended = attention_forward(
        doc_offsets, doc_lengths, tokens_in, qkv_pieces, pool_kernel, seq_len
    )
    rest_pieces = with_last(rest_pieces, attended)
    block_out, grad_att, grad_sum1, *terms, smalls = token_part(
        attended,
        hidden_in,
        cotangent,
        rest_pieces,
        (norm1_gain, norm1_bias, up_bias, down_bias, norm2_gain, norm2_bias),
    )
    shape = (rows, tokens, width)
    count = lax.axis_size("seq")
    bits = "xlhijk"[: count.bit_length() - 1]
    wide = (2,) * (len(bits) + 1) + (width // count, width)
    down_sent, down_kept, up_sent, up_kept, qkv_sent, qkv_kept = terms
    down_got = swapped(down_sent, "c").reshape(wide)
    up_got = swapped(up_sent, "c").reshape(wide)
    run = Order(smalls)
    common = (doc_offsets, doc_lengths, tokens_in, pool_kernel, saved, seq_len)
    last = len(bits)

    qkv_sent, qkv_kept, dpool_a, dq_a, dkv_a = run(
        attention_backward, grad_att.reshape(shape), qkv_sent, qkv_kept, *common, (0, 1)
    )
    down_sent, down_kept = run(split, down_kept.reshape(wide), down_got, 0, "y")
    down_got = swapped(down_sent, "y")
    up_sent, up_kept = run(split, up_kept.reshape(wide), up_got, last - 1, "l")
    up_got = swapped(up_sent, "l")
    qkv_sent, qkv_kept, dpool_b, dq_b, dkv_b = run(
        attention_backward, grad_att.reshape(shape), qkv_sent, qkv_kept, *common, (1, 2)
    )
    qkv_got = swapped(qkv_sent, "c").reshape(wide)
    small = jnp.concatenate(
        [jnp.concatenate([dpool_a, dpool_b], axis=2).reshape(10, width), smalls], axis=0
    )
    small_got = swapped(small, "c")
    down_sent, down_kept = run(split, down_kept, down_got, last - 2, "l")
    down_got = swapped(down_sent, "l")
    up_sent, up_kept = run(split, up_kept, up_got, 0, "y")
    up_got = swapped(up_sent, "y")
    dx_own, dx_ll, dx_l, dx_r = run(
        input_gradient, grad_sum1.reshape(shape), qkv_pieces, (dq_a, dq_b), (dkv_a, dkv_b)
    )
    dx_parts = (moved(dx_l, -1), moved(dx_r, 1), moved(dx_ll, -2))
    qkv_sent, qkv_kept = run(split, qkv_kept.reshape(wide), qkv_got, 0, "y")
    qkv_got = swapped(qkv_sent, "y")
    small = small + small_got
    small_got = swapped(small, "y")

    both_kept = jnp.concatenate([down_kept, up_kept], axis=-2)
    both_got = jnp.concatenate([down_got, up_got], axis=-2)
    names = ["x", *bits[2:]]
    for name in names:
        both_sent, both_kept = run(split, both_kept, both_got, both_kept.ndim - 3, name)
        both_got = swapped(both_sent, name)
    qkv_sent, qkv_kept = run(split, qkv_kept, qkv_got, last - 1, "x")
    qkv_got = swapped(qkv_sent, "x")
    small = small + small_got
    small_got = swapped(small, "x")
    (both,) = run(summed, both_kept, both_got)
    both_got = swapped(both, names[-1])
    qkv_sent, qkv_kept = run(split, qkv_kept, qkv_got, last - 2, "l")
    qkv_got = swapped(qkv_sent, "l")
    small = small + small_got
    small_got = swapped(small, "l")
    for index, name in enumerate(names[::-1]):
        (both,) = run(joined, both, both_got, both.ndim - 2, name)
        both_got = swapped(both, (names[::-1] + ["l"])[index + 1])
    for name in bits[2:]:
        qkv_sent, qkv_kept = run(split, qkv_kept, qkv_got, qkv_kept.ndim - 3, name)
        qkv_got = swapped(qkv_sent, name)
        small = small + small_got
        small_got = swapped(small, name)
    (grad_in,) = run(input_sum, dx_own, *dx_parts)
    (qkv,) = run(summed, qkv_kept, qkv_got)
    small = small + small_got
    qkv_got = swapped(qkv, bits[-1])
    (both,) = run(joined, both, both_got, both.ndim - 3, "l", F32)
    for index, name in enumerate(bits[:0:-1]):
        (qkv,) = run(joined, qkv, qkv_got, qkv.ndim - 2, name)
        qkv_got = swapped(qkv, bits[last - 2 - index])
    (qkv,) = run(joined, qkv, qkv_got, qkv.ndim - 2, "x", F32)

    def side_by_side(cells):
        parts = cells.size // (quarter * width)
        cells = cells.reshape(parts, quarter, width).transpose(1, 0, 2)
        return cells.reshape(quarter, parts * width)

    per = width // count
    both = both.reshape(count, 2, per, width)
    grad_down = both[:, 0].reshape(width, width)
    grad_up = side_by_side(both[:, 1])
    qkv = qkv.reshape(4, quarter, width)
    return (
        block_out.reshape(shape),
        grad_in,
        side_by_side(qkv[:3]),
        qkv[3],
        small[:10].reshape(2, 5, width),
        small[10],
        small[11],
        grad_up,
        small[15:].reshape(hidden),
        grad_down,
        small[12],
        small[13],
        small[14],
    )


def solution(mesh):
    placed = (
        P("dp", "seq", None),
        P("dp", "seq", None),
        P("dp", None),
        P("dp", None),
        P(),
        P(),
        P(),
        P("dp", None),
        P(),
        P("dp", None),
        P(),
        P(),
        P(),
        P("dp", None),
        P("dp", None),
    )
    return jax.shard_map(
        local,
        mesh=mesh,
        in_specs=placed,
        out_specs=(
            P("dp", "seq", None),
            P("dp", "seq", None),
            P("dp", None),
            P("dp", None),
            P(),
            P(),
            P(),
            P("dp", None),
            P(),
            P("dp", None),
            P(),
            P(),
            P(),
        ),
        check_vma=False,
    )
```
